32 devices in a mesh: groups: 2 (over y), gx: 16 (over z, x, core).
Axes of the slice: x: 2, y: 2, z: 4, core: 2. Of those that a mesh axis runs over, the one named last changes fastest.
Arguments:
- hidden: bfloat16 [64, 28672], P(('groups', 'gx')), parts along dimension 0, may hold values from -6 to 6
- shared_down_weight: bfloat16 [28672, 8192], P('gx'), may hold values from -0.03125 to 0.03125
- adapter_first_factors: bfloat16 [16, 64, 28672], P('gx'), may hold values from -0.03125 to 0.03125
- adapter_second_factors: bfloat16 [16, 64, 8192], P('gx'), may hold values from -0.375 to 0.375
- segment_row_counts: int32 [32], P('groups'), parts along dimension 0, may hold values from 1 to 4, 32 in all
- slot_tenant_owner: int32 [16], replicated, may hold values from 0 to 15, each once
Outputs:
- mixed: bfloat16 [64, 8192], P(('groups', 'gx')), parts along dimension 0
The draws below stay inside these ranges and needn't reach their ends.
There are 2 independent parts, one for each index of `groups`. The reference program is written for one: setup_inputs(seed, part) draws one part's arguments, and reference() takes and returns one part's arrays. A program takes and returns all parts, laid end to end along the dimension named above; an argument that names none is the same for every part. Nothing has to cross between parts.
Inputs may be any that keep to these rules, and one draw needn't show every extreme that they name: `segment_row_counts`: the entries sum to 32; the largest is exactly 4. `slot_tenant_owner`: each tenant appears once.
All inputs are finite; a program needn't handle non-finite values.
Results may differ from the reference program's by a relative error of at most 0.0031.
Values may be sent and summed in bfloat16 or wider, within the bound.
A program may use at most 128 MiB of HBM per device.

```python
import math
import jax
import jax.numpy as jnp
import numpy as np
from jax import lax

MODEL_WIDTH = 8192
HIDDEN_UNITS = 28672
ADAPTER_RANK = 64
ROWS = 32
TENANT_COUNT = 16
MOST = 4


def strengthened(drawn, stream_key, source, target, parts, factor):
    owner, partner = [(jnp.arange(drawn.shape[dim]) // (drawn.shape[dim] // parts)).reshape([-1 if axis == dim else 1 for axis in range(drawn.ndim)]) for dim in (source, target)]
    chosen = jax.random.permutation(stream_key, parts)[partner]
    strong = (owner == chosen) | (owner == (partner + parts // 2) % parts)
    return jnp.where(strong, factor * drawn, drawn)


def levels(stream_key, extent, split, smallest, largest):
    loudness, own = 1.0, jax.random.fold_in(stream_key, 6)
    for axis_at, shards_of in split:
        steps = jnp.exp(jax.random.uniform(jax.random.fold_in(own, axis_at), (shards_of,), jnp.float32, smallest / len(split), largest / len(split)))
        loudness = loudness * jnp.repeat(steps, extent[axis_at] // shards_of).reshape([-1 if axis == axis_at else 1 for axis in range(len(extent))])
    return loudness


def length_profile(number_of, total, bound, slope):
    weights = [(1 << 20) // math.isqrt(standing ** slope) + 1 for standing in range(2, number_of + 1)]
    spare, counts = total - bound - (number_of - 1), [1] * (number_of - 1)
    while spare > 0:
        candidates = [i for i in range(number_of - 1) if counts[i] < bound]
        mass, remaining = sum([weights[i] for i in candidates]), spare
        for i in candidates:
            more = min(bound - counts[i], max(1, remaining * weights[i] // mass), spare)
            counts[i] = counts[i] + more
            spare = spare - more
    return np.array([bound] + counts)


def ragged_sizes(stream_key, amount, total, bound, skew):
    if amount == 2:
        one = jax.random.randint(stream_key, (), max(1, total - bound), min(bound, total - 1) + 1)
        return jnp.stack([one, total - one])
    lengths = jnp.asarray(length_profile(amount, total, bound, skew), jnp.int32)
    couples = (amount - 1) // 2
    source_of, sink = lengths[1:1 + 2 * couples:2], lengths[2:2 + 2 * couples:2]
    margin = jnp.minimum(source_of - 1, bound - sink)
    moved = jax.random.randint(jax.random.fold_in(stream_key, 1), (couples,), 0, 1 << 20) % (margin + 1)
    lengths = lengths.at[1:1 + 2 * couples:2].set(source_of - moved).at[2:2 + 2 * couples:2].set(sink + moved)
    return lengths[jax.random.permutation(jax.random.fold_in(stream_key, 2), amount)]


def bell_draw(own_key, shape, deviation, limit, shards=(), kind=jnp.bfloat16):
    entries = jax.random.normal(own_key, shape, jnp.float32) * deviation
    if len(shards) > 0:
        entries = levels(own_key, shape, shards, -0.22, 0.18) * entries
    return jnp.clip(entries, min=-limit, max=limit).astype(kind)


def noise_with(stream_key, extent, deviation, bound, shards, heavy, held_as=jnp.bfloat16):
    result = deviation * jax.random.normal(stream_key, extent, jnp.float32)
    if shards:
        result = result * levels(stream_key, extent, shards, -0.22, 0.18)
    return jnp.clip(strengthened(result, jax.random.fold_in(stream_key, 3), *heavy), -bound, bound).astype(held_as)


def setup_inputs(seed: int = 0, part: int = 0) -> dict:
    splits = jax.random.split(jax.random.key(seed), 7)
    own_keys = jax.random.split(jax.random.fold_in(splits[6], part), 7)
    return {
        "hidden": noise_with(own_keys[0], (ROWS, HIDDEN_UNITS), 1.0, 6.0, ((0, 16),), (1, 0, 16, 2.0)),
        "shared_down_weight": bell_draw(splits[1], (HIDDEN_UNITS, MODEL_WIDTH), HIDDEN_UNITS ** -0.5, 0.03125, ((0, 16),)),
        "adapter_first_factors": bell_draw(splits[2], (TENANT_COUNT, ADAPTER_RANK, HIDDEN_UNITS), HIDDEN_UNITS ** -0.5, 0.03125, ((0, 16),)),
        "adapter_second_factors": bell_draw(splits[3], (TENANT_COUNT, ADAPTER_RANK, MODEL_WIDTH), (4 * ADAPTER_RANK) ** -0.5, 0.375, ((0, 16),)),
        "segment_row_counts": ragged_sizes(own_keys[4], TENANT_COUNT, ROWS, MOST, 2).astype(jnp.int32),
        "slot_tenant_owner": jax.random.permutation(splits[5], TENANT_COUNT).astype(jnp.int32),
    }


def reference(hidden, shared_down_weight, adapter_first_factors, adapter_second_factors, segment_row_counts, slot_tenant_owner):
    total_rows = hidden.shape[0]
    seg_ends = jnp.cumsum(segment_row_counts).astype(jnp.int32)
    seg_starts = (seg_ends - segment_row_counts).astype(jnp.int32)
    row_index = jnp.arange(total_rows, dtype=jnp.int32)
    row_tenant = jnp.sum((seg_ends[None, :] <= row_index[:, None]).astype(jnp.int32), axis=1).astype(jnp.int32)
    tenant_index = jnp.arange(TENANT_COUNT, dtype=jnp.int32)
    slot_lookup = jnp.sum(jnp.where(slot_tenant_owner[None, :] == tenant_index[:, None], tenant_index[None, :], 0), axis=1).astype(jnp.int32)
    windows = jnp.minimum(seg_starts, total_rows - MOST).astype(jnp.int32)
    base_sum = jnp.dot(hidden, shared_down_weight, preferred_element_type=jnp.float32)

    def per_tenant(tenant):
        bank_slot_index = slot_lookup[tenant]
        window_rows = lax.dynamic_slice_in_dim(hidden, windows[tenant], MOST, 0).astype(jnp.float32)
        first_factor_bank = adapter_first_factors[bank_slot_index].astype(jnp.float32)
        rank_activations = lax.dot_general(window_rows, first_factor_bank, (((1,), (1,)), ((), ()))).astype(jnp.bfloat16)
        return jnp.dot(rank_activations, adapter_second_factors[bank_slot_index], preferred_element_type=jnp.float32)

    delta_all = lax.map(per_tenant, tenant_index)
    row_local = (row_index - windows[row_tenant]).astype(jnp.int32)
    delta_rows = delta_all[row_tenant, row_local]
    return (base_sum + delta_rows).astype(jnp.bfloat16)
```

```python
import functools

import jax
import jax.numpy as jnp
from jax import lax
from jax.experimental import pallas as pl
from jax.experimental.pallas import tpu as pltpu
from jax.sharding import PartitionSpec as P

MOST = 4
CHUNKS = 4
TILE = 512
MESH = pl.DeviceIdType.MESH


def kernel(
    n,
    counts_ref,
    owner_ref,
    hidden_ref,
    w_hbm,
    a1_hbm,
    a2_hbm,
    out_ref,
    wbuf,
    a1,
    a2,
    rows_in,
    xf,
    xb,
    onehot,
    win_out,
    win_in,
    part,
    pair_in,
    chip_sum,
    sum_out,
    sum_in,
    starts,
    w_sem,
    a_sem,
    s1,
    r1,
    s2,
    r2,
    s3,
    r3,
    s4,
    r4,
):
    me = lax.axis_index("gx")
    chip, core = me // 2, me % 2
    mate = chip * 2 + (1 - core)
    chips = n // 2
    rows_dev = hidden_ref.shape[0]
    rows = rows_dev * n
    half = rows // 2
    depth = w_hbm.shape[0]
    width = w_hbm.shape[1]
    cw = width // CHUNKS
    f32, bf16 = jnp.float32, jnp.bfloat16

    def w_copy(k):
        return pltpu.make_async_copy(w_hbm.at[:, pl.ds(k * cw, cw)], wbuf.at[k], w_sem.at[k])

    a1_copy = pltpu.make_async_copy(a1_hbm.at[0], a1, a_sem.at[0])
    a2_copy = pltpu.make_async_copy(a2_hbm.at[0], a2, a_sem.at[1])
    w_copy(0).start()
    a1_copy.start()
    a2_copy.start()
    for k in range(1, CHUNKS):
        w_copy(k).start()

    barrier = pltpu.get_barrier_semaphore()

    def greet(o, c):
        pl.semaphore_signal(barrier, inc=1, device_id={"gx": lax.rem(me + o, n)}, device_id_type=MESH)
        return c

    lax.fori_loop(1, n, greet, 0)
    pl.semaphore_wait(barrier, n - 1)

    def rows_copy(d, at):
        return pltpu.make_async_remote_copy(
            src_ref=hidden_ref.at[:, pl.ds(pl.multiple_of(d * depth, 128), depth)],
            dst_ref=rows_in.at[at],
            send_sem=s1.at[d],
            recv_sem=r1.at[at],
            device_id={"gx": d},
            device_id_type=MESH,
        )

    def send_rows(o, c):
        rows_copy(lax.rem(me + o, n), me).start()
        return c

    lax.fori_loop(1, n, send_rows, 0)
    rows_in[me] = hidden_ref[:, pl.ds(pl.multiple_of(me * depth, 128), depth)]

    total = jnp.int32(0)
    for t in range(n):
        starts[t] = total
        total = total + counts_ref[t]
    step = 8
    pos = lax.broadcasted_iota(jnp.int32, (step, rows), 1)
    row_at = ((pos % half) // rows_dev * 2 + pos // half) * rows_dev + pos % rows_dev
    nth = lax.broadcasted_iota(jnp.int32, (step, rows), 0)
    for s in range(n):
        t = owner_ref[s]
        hit = (row_at == starts[t] + nth) & (nth < counts_ref[t])
        onehot[s * step : (s + 1) * step, :] = jnp.where(hit, 1.0, 0.0).astype(f32)

    def wait_rows(o, c):
        s = lax.rem(me + o, n)
        rows_copy(s, s).wait_recv()
        return c

    lax.fori_loop(1, n, wait_rows, 0)
    for s in range(n):
        at = (s % 2) * half + (s // 2) * rows_dev
        xf[at : at + rows_dev, :] = rows_in[s].astype(f32)
    xb[...] = xf[...].astype(bf16)

    chosen = jnp.dot(onehot[...].astype(bf16), xb[...], preferred_element_type=f32)
    for s in range(n):
        win_out[s] = chosen[s * step : s * step + MOST, :].astype(bf16)

    def win_copy(d, at):
        return pltpu.make_async_remote_copy(
            src_ref=win_out.at[d],
            dst_ref=win_in.at[at],
            send_sem=s2.at[d],
            recv_sem=r2.at[at],
            device_id={"gx": d},
            device_id_type=MESH,
        )

    def send_win(o, c):
        win_copy(lax.rem(me + o, n), me).start()
        return c

    lax.fori_loop(1, n, send_win, 0)
    win_in[me] = win_out[me]

    def base(k):
        w_copy(k).wait()

        def tile(i, c):
            cols = pl.ds(pl.multiple_of(i * TILE, TILE), TILE)
            part[k, :, cols] = jnp.dot(xb[...], wbuf[k, :, cols], preferred_element_type=f32)
            return c

        lax.fori_loop(0, cw // TILE, tile, 0)

    base(0)
    base(1)

    a1_copy.wait()

    def wait_win(o, c):
        s = lax.rem(me + o, n)
        win_copy(s, s).wait_recv()
        return c

    lax.fori_loop(1, n, wait_win, 0)

    def shrink(s, acc):
        return acc + lax.dot_general(
            win_in[s],
            a1[:, pl.ds(pl.multiple_of(s * depth, 128), depth)],
            (((1,), (1,)), ((), ())),
            preferred_element_type=f32,
        )

    rank = a1.shape[0]
    low = lax.fori_loop(0, n, shrink, jnp.zeros((MOST, rank), f32))
    low = low.astype(bf16).astype(f32)
    tenant = owner_ref[me]
    pos = lax.broadcasted_iota(jnp.int32, (rows, rank), 0)
    row_at = ((pos % half) // rows_dev * 2 + pos // half) * rows_dev + pos % rows_dev
    spread = jnp.zeros((rows, rank), f32)
    for j in range(MOST):
        hit = (row_at == starts[tenant] + j) & (j < counts_ref[tenant])
        spread = jnp.where(hit, jnp.broadcast_to(low[j : j + 1, :], (rows, rank)), spread)
    spread = spread.astype(bf16)
    a2_copy.wait()

    mine = pl.ds(pl.multiple_of(core * half, 8), half)
    other = pl.ds(pl.multiple_of((1 - core) * half, 8), half)

    def pair_copy(k):
        return pltpu.make_async_remote_copy(
            src_ref=part.at[k, other],
            dst_ref=pair_in.at[k],
            send_sem=s3.at[k],
            recv_sem=r3.at[k],
            device_id={"gx": mate},
            device_id_type=MESH,
        )

    def chip_copy(k, c, at):
        return pltpu.make_async_remote_copy(
            src_ref=sum_out.at[k, c],
            dst_ref=sum_in.at[k, at],
            send_sem=s4.at[k, c],
            recv_sem=r4.at[k, at],
            device_id={"gx": c * 2 + core},
            device_id_type=MESH,
        )

    def add_delta(k):
        def tile(i, c):
            cols = pl.ds(pl.multiple_of(i * TILE, TILE), TILE)
            from_a2 = pl.ds(pl.multiple_of(k * cw + i * TILE, TILE), TILE)
            part[k, :, cols] += jnp.dot(spread, a2[:, from_a2], preferred_element_type=f32)
            return c

        lax.fori_loop(0, cw // TILE, tile, 0)
        pair_copy(k).start()

    def to_chips(k):
        pair_copy(k).wait_recv()
        chip_sum[k] = part[k, mine, :] + pair_in[k]
        for c in range(chips):
            sum_out[k, c] = chip_sum[k, c * rows_dev : (c + 1) * rows_dev, :].astype(bf16)

        def send(o, x):
            chip_copy(k, lax.rem(chip + o, chips), chip).start()
            return x

        lax.fori_loop(1, chips, send, 0)
        sum_in[k, chip] = jnp.zeros(sum_in.shape[2:], bf16)

    def finish(k):
        def wait(o, x):
            c = lax.rem(chip + o, chips)
            chip_copy(k, c, c).wait_recv()
            return x

        lax.fori_loop(1, chips, wait, 0)
        own = jnp.zeros((rows_dev, cw), f32)
        for c in range(chips):
            own += jnp.where(c == chip, chip_sum[k, c * rows_dev : (c + 1) * rows_dev, :], 0.0)
            own += sum_in[k, c].astype(f32)
        out_ref[:, k * cw : (k + 1) * cw] = own.astype(bf16)

    add_delta(0)
    add_delta(1)
    to_chips(0)
    to_chips(1)
    for k in range(2, CHUNKS):
        base(k)
        add_delta(k)
        to_chips(k)
    for k in range(CHUNKS):
        finish(k)

    def drain(o, c):
        d = lax.rem(me + o, n)
        rows_copy(d, me).wait_send()
        win_copy(d, me).wait_send()
        return c

    lax.fori_loop(1, n, drain, 0)

    for k in range(CHUNKS):
        pair_copy(k).wait_send()

        def drain_chips(o, x, k=k):
            chip_copy(k, lax.rem(chip + o, chips), chip).wait_send()
            return x

        lax.fori_loop(1, chips, drain_chips, 0)


def fused(hidden, shared_down_weight, adapter_first_factors, adapter_second_factors, segment_row_counts, slot_tenant_owner):
    n = lax.axis_size("gx")
    rows_dev = hidden.shape[0]
    rows = rows_dev * n
    depth, width = shared_down_weight.shape
    rank = adapter_first_factors.shape[1]
    cw = width // CHUNKS
    chips = n // 2
    bf16, f32 = jnp.bfloat16, jnp.float32
    dma = pltpu.SemaphoreType.DMA
    vmem = pl.BlockSpec(memory_space=pltpu.VMEM)
    smem = pl.BlockSpec(memory_space=pltpu.SMEM)
    hbm = pl.BlockSpec(memory_space=pltpu.HBM)
    return pl.pallas_call(
        functools.partial(kernel, n),
        out_shape=jax.ShapeDtypeStruct((rows_dev, width), bf16),
        in_specs=[smem, smem, vmem, hbm, hbm, hbm],
        out_specs=vmem,
        scratch_shapes=[
            pltpu.VMEM((CHUNKS, depth, cw), bf16),
            pltpu.VMEM(adapter_first_factors.shape[1:], bf16),
            pltpu.VMEM(adapter_second_factors.shape[1:], bf16),
            pltpu.VMEM((n, rows_dev, depth), bf16),
            pltpu.VMEM((rows, depth), f32),
            pltpu.VMEM((rows, depth), bf16),
            pltpu.VMEM((n * 8, rows), f32),
            pltpu.VMEM((n, MOST, depth), bf16),
            pltpu.VMEM((n, MOST, depth), bf16),
            pltpu.VMEM((CHUNKS, rows, cw), f32),
            pltpu.VMEM((CHUNKS, rows // 2, cw), f32),
            pltpu.VMEM((CHUNKS, rows // 2, cw), f32),
            pltpu.VMEM((CHUNKS, chips, rows_dev, cw), bf16),
            pltpu.VMEM((CHUNKS, chips, rows_dev, cw), bf16),
            pltpu.SMEM((n,), jnp.int32),
            dma((CHUNKS,)),
            dma((2,)),
            dma((n,)),
            dma((n,)),
            dma((n,)),
            dma((n,)),
            dma((CHUNKS,)),
            dma((CHUNKS,)),
            dma((CHUNKS, chips)),
            dma((CHUNKS, chips)),
        ],
        compiler_params=pltpu.CompilerParams(
            collective_id=0, has_side_effects=True, vmem_limit_bytes=56 * 2**20
        ),
        cost_estimate=pl.CostEstimate(
            flops=2 * rows * depth * width,
            bytes_accessed=2 * (depth * width + rank * (depth * n + width)),
            transcendentals=0,
        ),
    )(
        segment_row_counts,
        slot_tenant_owner,
        hidden,
        shared_down_weight,
        adapter_first_factors,
        adapter_second_factors,
    )


def general(
    hidden,
    shared_down_weight,
    adapter_first_factors,
    adapter_second_factors,
    segment_row_counts,
    slot_tenant_owner,
):
    devices = lax.axis_size("gx")
    own_index = lax.axis_index("gx")
    rows_dev = hidden.shape[0]
    total_rows = rows_dev * devices
    hidden_features_local = lax.all_to_all(hidden, "gx", split_axis=1, concat_axis=0, tiled=True)
    seg_ends = jnp.cumsum(segment_row_counts)
    seg_starts = seg_ends - segment_row_counts
    row_index = jnp.arange(total_rows, dtype=jnp.int32)
    row_tenant = jnp.sum((seg_ends[None, :] <= row_index[:, None]).astype(jnp.int32), axis=1)
    windows = jnp.minimum(seg_starts, total_rows - MOST)
    row_local = row_index - windows[row_tenant]

    def take_window(first_row):
        return lax.dynamic_slice_in_dim(hidden_features_local, first_row, MOST, 0)

    slot_blocks = jax.vmap(take_window)(windows[slot_tenant_owner])
    tenant_first_factor = adapter_first_factors[0]
    tenant_second_factor = adapter_second_factors[0]
    shrunk = lax.dot_general(
        lax.all_to_all(slot_blocks, "gx", split_axis=0, concat_axis=2, tiled=True),
        tenant_first_factor,
        (((2,), (1,)), ((), ())),
        preferred_element_type=jnp.float32,
    )
    shrunk = shrunk.astype(jnp.bfloat16)
    owned_delta = lax.dot_general(
        shrunk, tenant_second_factor, (((2,), (0,)), ((), ())), preferred_element_type=jnp.float32
    )[0]
    own_tenant = slot_tenant_owner[own_index]
    in_segment = (row_tenant == own_tenant).astype(jnp.float32)
    adapter_output_part = (
        jnp.take(owned_delta, jnp.clip(row_local, 0, MOST - 1), axis=0) * in_segment[:, None]
    )
    summed = lax.psum_scatter(
        jnp.dot(hidden_features_local, shared_down_weight, preferred_element_type=jnp.float32)
        + adapter_output_part,
        "gx",
        scatter_dimension=0,
        tiled=True,
    )
    return summed.astype(jnp.bfloat16)


def per_device(hidden, shared_down_weight, *rest):
    n = lax.axis_size("gx")
    depth, width = shared_down_weight.shape
    aligned = depth % 128 == 0 and width % (CHUNKS * TILE) == 0 and (hidden.shape[0] * n) % 32 == 0
    if aligned and n <= 16:
        return fused(hidden, shared_down_weight, *rest)
    return general(hidden, shared_down_weight, *rest)


def solution(mesh):
    return jax.shard_map(
        per_device,
        mesh=mesh,
        in_specs=(
            P(("groups", "gx"), None),
            P("gx", None),
            P("gx", None, None),
            P("gx", None, None),
            P("groups"),
            P(),
        ),
        out_specs=P(("groups", "gx"), None),
        check_vma=False,
    )
```

```python
import functools

import jax
import jax.numpy as jnp
from jax import lax
from jax.experimental import pallas as pl
from jax.experimental.pallas import tpu as pltpu
from jax.sharding import PartitionSpec as P

MOST = 4
CHUNKS = 4
TILE = 512
MESH = pl.DeviceIdType.MESH


def kernel(
    n,
    counts_ref,
    owner_ref,
    hidden_ref,
    w_hbm,
    a1_hbm,
    a2_hbm,
    out_ref,
    wbuf,
    a1,
    a2,
    rows_in,
    xf,
    xb,
    onehot,
    win_out,
    win_in,
    part,
    pair_in,
    chip_sum,
    sum_out,
    sum_in,
    starts,
    w_sem,
    a_sem,
    s1,
    r1,
    s2,
    r2,
    s3,
    r3,
    s4,
    r4,
    s5,
    r5,
    low_pair,
):
    me = lax.axis_index("gx")
    chip, core = me // 2, me % 2
    mate = chip * 2 + (1 - core)
    chips = n // 2
    rows_dev = hidden_ref.shape[0]
    rows = rows_dev * n
    half = rows // 2
    depth = w_hbm.shape[0]
    width = w_hbm.shape[1]
    cw = width // CHUNKS
    f32, bf16 = jnp.float32, jnp.bfloat16

    def w_copy(k):
        return pltpu.make_async_copy(w_hbm.at[:, pl.ds(k * cw, cw)], wbuf.at[k], w_sem.at[k])

    a1_copy = pltpu.make_async_copy(a1_hbm.at[0], a1, a_sem.at[0])
    rank = a1.shape[0]
    own_a2 = pl.ds(pl.multiple_of(core * rank, 16), rank)
    mate_a2 = pl.ds(pl.multiple_of((1 - core) * rank, 16), rank)
    a2_copy = pltpu.make_async_copy(a2_hbm.at[0], a2.at[own_a2], a_sem.at[1])
    w_copy(0).start()
    a1_copy.start()
    a2_copy.start()
    for k in range(1, CHUNKS):
        w_copy(k).start()

    barrier = pltpu.get_barrier_semaphore()

    def greet(o, c):
        pl.semaphore_signal(barrier, inc=1, device_id={"gx": lax.rem(me + o, n)}, device_id_type=MESH)
        return c

    lax.fori_loop(1, n, greet, 0)
    pl.semaphore_wait(barrier, n - 1)

    def rows_copy(d, at):
        return pltpu.make_async_remote_copy(
            src_ref=hidden_ref.at[:, pl.ds(pl.multiple_of(d * depth, 128), depth)],
            dst_ref=rows_in.at[at],
            send_sem=s1.at[d],
            recv_sem=r1.at[at],
            device_id={"gx": d},
            device_id_type=MESH,
        )

    def send_rows(o, c):
        rows_copy(lax.rem(me + o, n), me).start()
        return c

    lax.fori_loop(1, n, send_rows, 0)
    rows_in[me] = hidden_ref[:, pl.ds(pl.multiple_of(me * depth, 128), depth)]

    a2_send = pltpu.make_async_remote_copy(
        src_ref=a2_hbm.at[0],
        dst_ref=a2.at[own_a2],
        send_sem=s5.at[0],
        recv_sem=r5.at[0],
        device_id={"gx": mate},
        device_id_type=MESH,
    )
    a2_recv = pltpu.make_async_remote_copy(
        src_ref=a2_hbm.at[0],
        dst_ref=a2.at[mate_a2],
        send_sem=s5.at[0],
        recv_sem=r5.at[0],
        device_id={"gx": mate},
        device_id_type=MESH,
    )
    a2_send.start()

    total = jnp.int32(0)
    for t in range(n):
        starts[t] = total
        total = total + counts_ref[t]
    step = 8
    pos = lax.broadcasted_iota(jnp.int32, (step, rows), 1)
    row_at = ((pos % half) // rows_dev * 2 + pos // half) * rows_dev + pos % rows_dev
    nth = lax.broadcasted_iota(jnp.int32, (step, rows), 0)
    for s in range(n):
        t = owner_ref[s]
        hit = (row_at == starts[t] + nth) & (nth < counts_ref[t])
        onehot[s * step : (s + 1) * step, :] = jnp.where(hit, 1.0, 0.0).astype(f32)

    def wait_rows(o, c):
        s = lax.rem(me + o, n)
        rows_copy(s, s).wait_recv()
        return c

    lax.fori_loop(1, n, wait_rows, 0)
    for s in range(n):
        at = (s % 2) * half + (s // 2) * rows_dev
        xf[at : at + rows_dev, :] = rows_in[s].astype(f32)
    xb[...] = xf[...].astype(bf16)

    chosen = jnp.dot(onehot[...].astype(bf16), xb[...], preferred_element_type=f32)
    for s in range(n):
        win_out[s] = chosen[s * step : s * step + MOST, :].astype(bf16)

    def win_copy(d, at):
        return pltpu.make_async_remote_copy(
            src_ref=win_out.at[d],
            dst_ref=win_in.at[at],
            send_sem=s2.at[d],
            recv_sem=r2.at[at],
            device_id={"gx": d},
            device_id_type=MESH,
        )

    def send_win(o, c):
        win_copy(lax.rem(me + o, n), me).start()
        return c

    lax.fori_loop(1, n, send_win, 0)
    win_in[me] = win_out[me]

    def base(k):
        w_copy(k).wait()

        def tile(i, c):
            cols = pl.ds(pl.multiple_of(i * TILE, TILE), TILE)
            part[k, :, cols] = jnp.dot(xb[...], wbuf[k, :, cols], preferred_element_type=f32)
            return c

        lax.fori_loop(0, cw // TILE, tile, 0)

    mine = pl.ds(pl.multiple_of(core * half, 8), half)
    other = pl.ds(pl.multiple_of((1 - core) * half, 8), half)

    def pair_copy(k):
        return pltpu.make_async_remote_copy(
            src_ref=part.at[k, other],
            dst_ref=pair_in.at[k],
            send_sem=s3.at[k],
            recv_sem=r3.at[k],
            device_id={"gx": mate},
            device_id_type=MESH,
        )

    for k in range(CHUNKS):
        base(k)
        pair_copy(k).start()
    for k in range(CHUNKS):
        pair_copy(k).wait_recv()
        chip_sum[k] = part[k, mine, :] + pair_in[k]

    a1_copy.wait()

    def wait_win(o, c):
        s = lax.rem(me + o, n)
        win_copy(s, s).wait_recv()
        return c

    lax.fori_loop(1, n, wait_win, 0)
    low = jnp.zeros((rank, MOST), f32)
    for s in range(n):
        low += lax.dot_general(
            a1[:, s * depth : (s + 1) * depth],
            win_in[s],
            (((1,), (1,)), ((), ())),
            preferred_element_type=f32,
        )

    wide = 2 * rank
    lane = lax.broadcasted_iota(jnp.int32, (rank, wide), 1)
    unit = lax.broadcasted_iota(jnp.int32, (rank, wide), 0)
    place = jnp.where(lane == unit + core * rank, 1.0, 0.0).astype(bf16)
    low_pair[core] = lax.dot_general(
        low.astype(bf16), place, (((0,), (0,)), ((), ())), preferred_element_type=f32
    )
    low_send = pltpu.make_async_remote_copy(
        src_ref=low_pair.at[core],
        dst_ref=low_pair.at[core],
        send_sem=s5.at[1],
        recv_sem=r5.at[1],
        device_id={"gx": mate},
        device_id_type=MESH,
    )
    low_recv = pltpu.make_async_remote_copy(
        src_ref=low_pair.at[1 - core],
        dst_ref=low_pair.at[1 - core],
        send_sem=s5.at[1],
        recv_sem=r5.at[1],
        device_id={"gx": mate},
        device_id_type=MESH,
    )
    low_send.start()
    a2_copy.wait()
    a2_recv.wait_recv()
    pos = lax.broadcasted_iota(jnp.int32, (half, wide), 0)
    lane = lax.broadcasted_iota(jnp.int32, (half, wide), 1)
    row_at = (pos // rows_dev * 2 + core) * rows_dev + pos % rows_dev
    even, odd = owner_ref[chip * 2], owner_ref[chip * 2 + 1]
    first = jnp.where(lane < rank, starts[even], starts[odd])
    many = jnp.where(lane < rank, counts_ref[even], counts_ref[odd])
    low_recv.wait_recv()
    low = low_pair[0] + low_pair[1]
    spread = jnp.zeros((half, wide), f32)
    for j in range(MOST):
        hit = (row_at == first + j) & (j < many)
        spread = jnp.where(hit, jnp.broadcast_to(low[j : j + 1, :], (half, wide)), spread)
    spread = spread.astype(bf16)

    def chip_copy(k, c, at):
        return pltpu.make_async_remote_copy(
            src_ref=sum_out.at[k, c],
            dst_ref=sum_in.at[k, at],
            send_sem=s4.at[k, c],
            recv_sem=r4.at[k, at],
            device_id={"gx": c * 2 + core},
            device_id_type=MESH,
        )

    def to_chips(k):
        def tile(i, c):
            cols = pl.ds(pl.multiple_of(i * TILE, TILE), TILE)
            from_a2 = pl.ds(pl.multiple_of(k * cw + i * TILE, TILE), TILE)
            chip_sum[k, :, cols] += jnp.dot(spread, a2[:, from_a2], preferred_element_type=f32)
            return c

        lax.fori_loop(0, cw // TILE, tile, 0)
        for c in range(chips):
            sum_out[k, c] = chip_sum[k, c * rows_dev : (c + 1) * rows_dev, :].astype(bf16)

        def send(o, x):
            chip_copy(k, lax.rem(chip + o, chips), chip).start()
            return x

        lax.fori_loop(1, chips, send, 0)
        sum_in[k, chip] = jnp.zeros(sum_in.shape[2:], bf16)

    def finish(k):
        def wait(o, x):
            c = lax.rem(chip + o, chips)
            chip_copy(k, c, c).wait_recv()
            return x

        lax.fori_loop(1, chips, wait, 0)
        own = jnp.zeros((rows_dev, cw), f32)
        for c in range(chips):
            own += jnp.where(c == chip, chip_sum[k, c * rows_dev : (c + 1) * rows_dev, :], 0.0)
            own += sum_in[k, c].astype(f32)
        out_ref[:, k * cw : (k + 1) * cw] = own.astype(bf16)

    for k in range(CHUNKS):
        to_chips(k)
    for k in range(CHUNKS):
        finish(k)

    def drain(o, c):
        d = lax.rem(me + o, n)
        rows_copy(d, me).wait_send()
        win_copy(d, me).wait_send()
        return c

    lax.fori_loop(1, n, drain, 0)

    a2_send.wait_send()
    low_send.wait_send()
    for k in range(CHUNKS):
        pair_copy(k).wait_send()

        def drain_chips(o, x, k=k):
            chip_copy(k, lax.rem(chip + o, chips), chip).wait_send()
            return x

        lax.fori_loop(1, chips, drain_chips, 0)


def fused(hidden, shared_down_weight, adapter_first_factors, adapter_second_factors, segment_row_counts, slot_tenant_owner):
    n = lax.axis_size("gx")
    rows_dev = hidden.shape[0]
    rows = rows_dev * n
    depth, width = shared_down_weight.shape
    rank = adapter_first_factors.shape[1]
    cw = width // CHUNKS
    chips = n // 2
    bf16, f32 = jnp.bfloat16, jnp.float32
    dma = pltpu.SemaphoreType.DMA
    vmem = pl.BlockSpec(memory_space=pltpu.VMEM)
    smem = pl.BlockSpec(memory_space=pltpu.SMEM)
    hbm = pl.BlockSpec(memory_space=pltpu.HBM)
    return pl.pallas_call(
        functools.partial(kernel, n),
        out_shape=jax.ShapeDtypeStruct((rows_dev, width), bf16),
        in_specs=[smem, smem, vmem, hbm, hbm, hbm],
        out_specs=vmem,
        scratch_shapes=[
            pltpu.VMEM((CHUNKS, depth, cw), bf16),
            pltpu.VMEM(adapter_first_factors.shape[1:], bf16),
            pltpu.VMEM((2 * rank, width), bf16),
            pltpu.VMEM((n, rows_dev, depth), bf16),
            pltpu.VMEM((rows, depth), f32),
            pltpu.VMEM((rows, depth), bf16),
            pltpu.VMEM((n * 8, rows), f32),
            pltpu.VMEM((n, MOST, depth), bf16),
            pltpu.VMEM((n, MOST, depth), bf16),
            pltpu.VMEM((CHUNKS, rows, cw), f32),
            pltpu.VMEM((CHUNKS, rows // 2, cw), f32),
            pltpu.VMEM((CHUNKS, rows // 2, cw), f32),
            pltpu.VMEM((CHUNKS, chips, rows_dev, cw), bf16),
            pltpu.VMEM((CHUNKS, chips, rows_dev, cw), bf16),
            pltpu.SMEM((n,), jnp.int32),
            dma((CHUNKS,)),
            dma((2,)),
            dma((n,)),
            dma((n,)),
            dma((n,)),
            dma((n,)),
            dma((CHUNKS,)),
            dma((CHUNKS,)),
            dma((CHUNKS, chips)),
            dma((CHUNKS, chips)),
            dma((2,)),
            dma((2,)),
            pltpu.VMEM((2, MOST, 2 * rank), f32),
        ],
        compiler_params=pltpu.CompilerParams(
            collective_id=0, has_side_effects=True, vmem_limit_bytes=56 * 2**20
        ),
        cost_estimate=pl.CostEstimate(
            flops=2 * rows * depth * width,
            bytes_accessed=2 * (depth * width + rank * (depth * n + width)),
            transcendentals=0,
        ),
    )(
        segment_row_counts,
        slot_tenant_owner,
        hidden,
        shared_down_weight,
        adapter_first_factors,
        adapter_second_factors,
    )


def general(
    hidden,
    shared_down_weight,
    adapter_first_factors,
    adapter_second_factors,
    segment_row_counts,
    slot_tenant_owner,
):
    devices = lax.axis_size("gx")
    own_index = lax.axis_index("gx")
    rows_dev = hidden.shape[0]
    total_rows = rows_dev * devices
    hidden_features_local = lax.all_to_all(hidden, "gx", split_axis=1, concat_axis=0, tiled=True)
    seg_ends = jnp.cumsum(segment_row_counts)
    seg_starts = seg_ends - segment_row_counts
    row_index = jnp.arange(total_rows, dtype=jnp.int32)
    row_tenant = jnp.sum((seg_ends[None, :] <= row_index[:, None]).astype(jnp.int32), axis=1)
    windows = jnp.minimum(seg_starts, total_rows - MOST)
    row_local = row_index - windows[row_tenant]

    def take_window(first_row):
        return lax.dynamic_slice_in_dim(hidden_features_local, first_row, MOST, 0)

    slot_blocks = jax.vmap(take_window)(windows[slot_tenant_owner])
    tenant_first_factor = adapter_first_factors[0]
    tenant_second_factor = adapter_second_factors[0]
    shrunk = lax.dot_general(
        lax.all_to_all(slot_blocks, "gx", split_axis=0, concat_axis=2, tiled=True),
        tenant_first_factor,
        (((2,), (1,)), ((), ())),
        preferred_element_type=jnp.float32,
    )
    shrunk = shrunk.astype(jnp.bfloat16)
    owned_delta = lax.dot_general(
        shrunk, tenant_second_factor, (((2,), (0,)), ((), ())), preferred_element_type=jnp.float32
    )[0]
    own_tenant = slot_tenant_owner[own_index]
    in_segment = (row_tenant == own_tenant).astype(jnp.float32)
    adapter_output_part = (
        jnp.take(owned_delta, jnp.clip(row_local, 0, MOST - 1), axis=0) * in_segment[:, None]
    )
    summed = lax.psum_scatter(
        jnp.dot(hidden_features_local, shared_down_weight, preferred_element_type=jnp.float32)
        + adapter_output_part,
        "gx",
        scatter_dimension=0,
        tiled=True,
    )
    return summed.astype(jnp.bfloat16)


def per_device(hidden, shared_down_weight, *rest):
    n = lax.axis_size("gx")
    depth, width = shared_down_weight.shape
    aligned = depth % 128 == 0 and width % (CHUNKS * TILE) == 0 and (hidden.shape[0] * n) % 32 == 0
    if aligned and n <= 16 and rest[0].shape[1] % 64 == 0:
        return fused(hidden, shared_down_weight, *rest)
    return general(hidden, shared_down_weight, *rest)


def solution(mesh):
    return jax.shard_map(
        per_device,
        mesh=mesh,
        in_specs=(
            P(("groups", "gx"), None),
            P("gx", None),
            P("gx", None, None),
            P("gx", None, None),
            P("groups"),
            P(),
        ),
        out_specs=P(("groups", "gx"), None),
        check_vma=False,
    )
```

```python
import functools

import jax
import jax.numpy as jnp
from jax import lax
from jax.experimental import pallas as pl
from jax.experimental.pallas import tpu as pltpu
from jax.sharding import PartitionSpec as P

MOST = 4
CHUNKS = 2
TILE = 512
MESH = pl.DeviceIdType.MESH


def kernel(
    n,
    counts_ref,
    owner_ref,
    hidden_ref,
    w_hbm,
    a1_hbm,
    a2_hbm,
    out_ref,
    wbuf,
    a1,
    a2,
    rows_in,
    xf,
    xb,
    onehot,
    win_out,
    win_in,
    part,
    pair_in,
    chip_sum,
    sum_out,
    sum_in,
    starts,
    w_sem,
    a_sem,
    s1,
    r1,
    s2,
    r2,
    s3,
    r3,
    s4,
    r4,
    s5,
    r5,
    low_pair,
):
    me = lax.axis_index("gx")
    chip, core = me // 2, me % 2
    mate = chip * 2 + (1 - core)
    chips = n // 2
    rows_dev = hidden_ref.shape[0]
    rows = rows_dev * n
    half = rows // 2
    depth = w_hbm.shape[0]
    width = w_hbm.shape[1]
    cw = width // CHUNKS
    f32, bf16 = jnp.float32, jnp.bfloat16

    def w_copy(k):
        return pltpu.make_async_copy(w_hbm.at[:, pl.ds(k * cw, cw)], wbuf.at[k], w_sem.at[k])

    a1_copy = pltpu.make_async_copy(a1_hbm.at[0], a1, a_sem.at[0])
    rank = a1.shape[0]
    own_a2 = pl.ds(pl.multiple_of(core * rank, 16), rank)
    mate_a2 = pl.ds(pl.multiple_of((1 - core) * rank, 16), rank)
    a2_copy = pltpu.make_async_copy(a2_hbm.at[0], a2.at[own_a2], a_sem.at[1])
    w_copy(0).start()
    a1_copy.start()
    a2_copy.start()
    for k in range(1, CHUNKS):
        w_copy(k).start()

    barrier = pltpu.get_barrier_semaphore()

    def greet(o, c):
        pl.semaphore_signal(barrier, inc=1, device_id={"gx": lax.rem(me + o, n)}, device_id_type=MESH)
        return c

    lax.fori_loop(1, n, greet, 0)
    pl.semaphore_wait(barrier, n - 1)

    def rows_copy(d, at):
        return pltpu.make_async_remote_copy(
            src_ref=hidden_ref.at[:, pl.ds(pl.multiple_of(d * depth, 128), depth)],
            dst_ref=rows_in.at[at],
            send_sem=s1.at[d],
            recv_sem=r1.at[at],
            device_id={"gx": d},
            device_id_type=MESH,
        )

    def send_rows(o, c):
        rows_copy(lax.rem(me + o, n), me).start()
        return c

    lax.fori_loop(1, n, send_rows, 0)
    rows_in[me] = hidden_ref[:, pl.ds(pl.multiple_of(me * depth, 128), depth)]

    a2_send = pltpu.make_async_remote_copy(
        src_ref=a2_hbm.at[0],
        dst_ref=a2.at[own_a2],
        send_sem=s5.at[0],
        recv_sem=r5.at[0],
        device_id={"gx": mate},
        device_id_type=MESH,
    )
    a2_recv = pltpu.make_async_remote_copy(
        src_ref=a2_hbm.at[0],
        dst_ref=a2.at[mate_a2],
        send_sem=s5.at[0],
        recv_sem=r5.at[0],
        device_id={"gx": mate},
        device_id_type=MESH,
    )
    a2_send.start()

    total = jnp.int32(0)
    for t in range(n):
        starts[t] = total
        total = total + counts_ref[t]
    step = 8
    pos = lax.broadcasted_iota(jnp.int32, (step, rows), 1)
    row_at = ((pos % half) // rows_dev * 2 + pos // half) * rows_dev + pos % rows_dev
    nth = lax.broadcasted_iota(jnp.int32, (step, rows), 0)
    for s in range(n):
        t = owner_ref[s]
        hit = (row_at == starts[t] + nth) & (nth < counts_ref[t])
        onehot[s * step : (s + 1) * step, :] = jnp.where(hit, 1.0, 0.0).astype(f32)

    def wait_rows(o, c):
        s = lax.rem(me + o, n)
        rows_copy(s, s).wait_recv()
        return c

    lax.fori_loop(1, n, wait_rows, 0)
    for s in range(n):
        at = (s % 2) * half + (s // 2) * rows_dev
        xf[at : at + rows_dev, :] = rows_in[s].astype(f32)
    xb[...] = xf[...].astype(bf16)

    chosen = jnp.dot(onehot[...].astype(bf16), xb[...], preferred_element_type=f32)
    for s in range(n):
        win_out[s] = chosen[s * step : s * step + MOST, :].astype(bf16)

    def win_copy(d, at):
        return pltpu.make_async_remote_copy(
            src_ref=win_out.at[d],
            dst_ref=win_in.at[at],
            send_sem=s2.at[d],
            recv_sem=r2.at[at],
            device_id={"gx": d},
            device_id_type=MESH,
        )

    def send_win(o, c):
        win_copy(lax.rem(me + o, n), me).start()
        return c

    lax.fori_loop(1, n, send_win, 0)
    win_in[me] = win_out[me]

    def base(k):
        w_copy(k).wait()

        def tile(i, c):
            cols = pl.ds(pl.multiple_of(i * TILE, TILE), TILE)
            part[k, :, cols] = jnp.dot(xb[...], wbuf[k, :, cols], preferred_element_type=f32)
            return c

        lax.fori_loop(0, cw // TILE, tile, 0)

    mine = pl.ds(pl.multiple_of(core * half, 8), half)
    other = pl.ds(pl.multiple_of((1 - core) * half, 8), half)

    def pair_copy(k):
        return pltpu.make_async_remote_copy(
            src_ref=part.at[k, other],
            dst_ref=pair_in.at[k],
            send_sem=s3.at[k],
            recv_sem=r3.at[k],
            device_id={"gx": mate},
            device_id_type=MESH,
        )

    for k in range(CHUNKS):
        base(k)
        pair_copy(k).start()
    for k in range(CHUNKS):
        pair_copy(k).wait_recv()
        chip_sum[k] = part[k, mine, :] + pair_in[k]

    a1_copy.wait()

    def wait_win(o, c):
        s = lax.rem(me + o, n)
        win_copy(s, s).wait_recv()
        return c

    lax.fori_loop(1, n, wait_win, 0)
    low = jnp.zeros((rank, MOST), f32)
    for s in range(n):
        low += lax.dot_general(
            a1[:, s * depth : (s + 1) * depth],
            win_in[s],
            (((1,), (1,)), ((), ())),
            preferred_element_type=f32,
        )

    wide = 2 * rank
    lane = lax.broadcasted_iota(jnp.int32, (rank, wide), 1)
    unit = lax.broadcasted_iota(jnp.int32, (rank, wide), 0)
    place = jnp.where(lane == unit + core * rank, 1.0, 0.0).astype(bf16)
    low_pair[core] = lax.dot_general(
        low.astype(bf16), place, (((0,), (0,)), ((), ())), preferred_element_type=f32
    )
    low_send = pltpu.make_async_remote_copy(
        src_ref=low_pair.at[core],
        dst_ref=low_pair.at[core],
        send_sem=s5.at[1],
        recv_sem=r5.at[1],
        device_id={"gx": mate},
        device_id_type=MESH,
    )
    low_recv = pltpu.make_async_remote_copy(
        src_ref=low_pair.at[1 - core],
        dst_ref=low_pair.at[1 - core],
        send_sem=s5.at[1],
        recv_sem=r5.at[1],
        device_id={"gx": mate},
        device_id_type=MESH,
    )
    low_send.start()
    a2_copy.wait()
    a2_recv.wait_recv()
    pos = lax.broadcasted_iota(jnp.int32, (half, wide), 0)
    lane = lax.broadcasted_iota(jnp.int32, (half, wide), 1)
    row_at = (pos // rows_dev * 2 + core) * rows_dev + pos % rows_dev
    even, odd = owner_ref[chip * 2], owner_ref[chip * 2 + 1]
    first = jnp.where(lane < rank, starts[even], starts[odd])
    many = jnp.where(lane < rank, counts_ref[even], counts_ref[odd])
    low_recv.wait_recv()
    low = low_pair[0] + low_pair[1]
    spread = jnp.zeros((half, wide), f32)
    for j in range(MOST):
        hit = (row_at == first + j) & (j < many)
        spread = jnp.where(hit, jnp.broadcast_to(low[j : j + 1, :], (half, wide)), spread)
    spread = spread.astype(bf16)

    def chip_copy(k, c, at):
        return pltpu.make_async_remote_copy(
            src_ref=sum_out.at[k, c],
            dst_ref=sum_in.at[k, at],
            send_sem=s4.at[k, c],
            recv_sem=r4.at[k, at],
            device_id={"gx": c * 2 + core},
            device_id_type=MESH,
        )

    def to_chips(k):
        def tile(i, c):
            cols = pl.ds(pl.multiple_of(i * TILE, TILE), TILE)
            from_a2 = pl.ds(pl.multiple_of(k * cw + i * TILE, TILE), TILE)
            chip_sum[k, :, cols] += jnp.dot(spread, a2[:, from_a2], preferred_element_type=f32)
            return c

        lax.fori_loop(0, cw // TILE, tile, 0)
        for c in range(chips):
            sum_out[k, c] = chip_sum[k, c * rows_dev : (c + 1) * rows_dev, :].astype(bf16)

        def send(o, x):
            chip_copy(k, lax.rem(chip + o, chips), chip).start()
            return x

        lax.fori_loop(1, chips, send, 0)
        sum_in[k, chip] = jnp.zeros(sum_in.shape[2:], bf16)

    def finish(k):
        def wait(o, x):
            c = lax.rem(chip + o, chips)
            chip_copy(k, c, c).wait_recv()
            return x

        lax.fori_loop(1, chips, wait, 0)
        own = jnp.zeros((rows_dev, cw), f32)
        for c in range(chips):
            own += jnp.where(c == chip, chip_sum[k, c * rows_dev : (c + 1) * rows_dev, :], 0.0)
            own += sum_in[k, c].astype(f32)
        out_ref[:, k * cw : (k + 1) * cw] = own.astype(bf16)

    for k in range(CHUNKS):
        to_chips(k)
    for k in range(CHUNKS):
        finish(k)

    def drain(o, c):
        d = lax.rem(me + o, n)
        rows_copy(d, me).wait_send()
        win_copy(d, me).wait_send()
        return c

    lax.fori_loop(1, n, drain, 0)

    a2_send.wait_send()
    low_send.wait_send()
    for k in range(CHUNKS):
        pair_copy(k).wait_send()

        def drain_chips(o, x, k=k):
            chip_copy(k, lax.rem(chip + o, chips), chip).wait_send()
            return x

        lax.fori_loop(1, chips, drain_chips, 0)


def fused(hidden, shared_down_weight, adapter_first_factors, adapter_second_factors, segment_row_counts, slot_tenant_owner):
    n = lax.axis_size("gx")
    rows_dev = hidden.shape[0]
    rows = rows_dev * n
    depth, width = shared_down_weight.shape
    rank = adapter_first_factors.shape[1]
    cw = width // CHUNKS
    chips = n // 2
    bf16, f32 = jnp.bfloat16, jnp.float32
    dma = pltpu.SemaphoreType.DMA
    vmem = pl.BlockSpec(memory_space=pltpu.VMEM)
    smem = pl.BlockSpec(memory_space=pltpu.SMEM)
    hbm = pl.BlockSpec(memory_space=pltpu.HBM)
    return pl.pallas_call(
        functools.partial(kernel, n),
        out_shape=jax.ShapeDtypeStruct((rows_dev, width), bf16),
        in_specs=[smem, smem, vmem, hbm, hbm, hbm],
        out_specs=vmem,
        scratch_shapes=[
            pltpu.VMEM((CHUNKS, depth, cw), bf16),
            pltpu.VMEM(adapter_first_factors.shape[1:], bf16),
            pltpu.VMEM((2 * rank, width), bf16),
            pltpu.VMEM((n, rows_dev, depth), bf16),
            pltpu.VMEM((rows, depth), f32),
            pltpu.VMEM((rows, depth), bf16),
            pltpu.VMEM((n * 8, rows), f32),
            pltpu.VMEM((n, MOST, depth), bf16),
            pltpu.VMEM((n, MOST, depth), bf16),
            pltpu.VMEM((CHUNKS, rows, cw), f32),
            pltpu.VMEM((CHUNKS, rows // 2, cw), f32),
            pltpu.VMEM((CHUNKS, rows // 2, cw), f32),
            pltpu.VMEM((CHUNKS, chips, rows_dev, cw), bf16),
            pltpu.VMEM((CHUNKS, chips, rows_dev, cw), bf16),
            pltpu.SMEM((n,), jnp.int32),
            dma((CHUNKS,)),
            dma((2,)),
            dma((n,)),
            dma((n,)),
            dma((n,)),
            dma((n,)),
            dma((CHUNKS,)),
            dma((CHUNKS,)),
            dma((CHUNKS, chips)),
            dma((CHUNKS, chips)),
            dma((2,)),
            dma((2,)),
            pltpu.VMEM((2, MOST, 2 * rank), f32),
        ],
        compiler_params=pltpu.CompilerParams(
            collective_id=0, has_side_effects=True, vmem_limit_bytes=56 * 2**20
        ),
        cost_estimate=pl.CostEstimate(
            flops=2 * rows * depth * width,
            bytes_accessed=2 * (depth * width + rank * (depth * n + width)),
            transcendentals=0,
        ),
    )(
        segment_row_counts,
        slot_tenant_owner,
        hidden,
        shared_down_weight,
        adapter_first_factors,
        adapter_second_factors,
    )


def general(
    hidden,
    shared_down_weight,
    adapter_first_factors,
    adapter_second_factors,
    segment_row_counts,
    slot_tenant_owner,
):
    devices = lax.axis_size("gx")
    own_index = lax.axis_index("gx")
    rows_dev = hidden.shape[0]
    total_rows = rows_dev * devices
    hidden_features_local = lax.all_to_all(hidden, "gx", split_axis=1, concat_axis=0, tiled=True)
    seg_ends = jnp.cumsum(segment_row_counts)
    seg_starts = seg_ends - segment_row_counts
    row_index = jnp.arange(total_rows, dtype=jnp.int32)
    row_tenant = jnp.sum((seg_ends[None, :] <= row_index[:, None]).astype(jnp.int32), axis=1)
    windows = jnp.minimum(seg_starts, total_rows - MOST)
    row_local = row_index - windows[row_tenant]

    def take_window(first_row):
        return lax.dynamic_slice_in_dim(hidden_features_local, first_row, MOST, 0)

    slot_blocks = jax.vmap(take_window)(windows[slot_tenant_owner])
    tenant_first_factor = adapter_first_factors[0]
    tenant_second_factor = adapter_second_factors[0]
    shrunk = lax.dot_general(
        lax.all_to_all(slot_blocks, "gx", split_axis=0, concat_axis=2, tiled=True),
        tenant_first_factor,
        (((2,), (1,)), ((), ())),
        preferred_element_type=jnp.float32,
    )
    shrunk = shrunk.astype(jnp.bfloat16)
    owned_delta = lax.dot_general(
        shrunk, tenant_second_factor, (((2,), (0,)), ((), ())), preferred_element_type=jnp.float32
    )[0]
    own_tenant = slot_tenant_owner[own_index]
    in_segment = (row_tenant == own_tenant).astype(jnp.float32)
    adapter_output_part = (
        jnp.take(owned_delta, jnp.clip(row_local, 0, MOST - 1), axis=0) * in_segment[:, None]
    )
    summed = lax.psum_scatter(
        jnp.dot(hidden_features_local, shared_down_weight, preferred_element_type=jnp.float32)
        + adapter_output_part,
        "gx",
        scatter_dimension=0,
        tiled=True,
    )
    return summed.astype(jnp.bfloat16)


def per_device(hidden, shared_down_weight, *rest):
    n = lax.axis_size("gx")
    depth, width = shared_down_weight.shape
    aligned = depth % 128 == 0 and width % (CHUNKS * TILE) == 0 and (hidden.shape[0] * n) % 32 == 0
    if aligned and n <= 16 and rest[0].shape[1] % 64 == 0:
        return fused(hidden, shared_down_weight, *rest)
    return general(hidden, shared_down_weight, *rest)


def solution(mesh):
    return jax.shard_map(
        per_device,
        mesh=mesh,
        in_specs=(
            P(("groups", "gx"), None),
            P("gx", None),
            P("gx", None, None),
            P("gx", None, None),
            P("groups"),
            P(),
        ),
        out_specs=P(("groups", "gx"), None),
        check_vma=False,
    )
```
